128 devices in a mesh: rep: 4 (over z_hi, core), fsdp: 32 (over z_lo, x, y).
Axes of the slice: x: 4, y: 4, z: 4 (z_hi: 2, z_lo: 2; z = z_hi * 2 + z_lo), core: 2. Of those that a mesh axis runs over, the one named last changes fastest.
Arguments:
- in_table: bfloat16 [4, 256, 2048], P('rep'), may hold values from -6 to 6
- target_table: bfloat16 [4, 256, 2048], P('rep'), may hold values from -3 to 3
- in_ids: int32 [4, 4, 256], P('rep'), may hold values from 0 to 255
- target_ids: int32 [4, 4, 256], P('rep'), may hold values from 0 to 255
- gate_up: float32 [2, 2048, 14336], P(None, 'rep', 'fsdp'), may hold values from -6 to 6
- down: float32 [14336, 2048], P('fsdp', 'rep'), may hold values from -6 to 6
- mom_gate_up: float32 [2, 2048, 14336], P(None, 'rep', 'fsdp'), may hold values from -0.6 to 0.6
- mom_down: float32 [14336, 2048], P('fsdp', 'rep'), may hold values from -0.6 to 0.6
- m_gate_up: bfloat16 [4, 2, 2048, 14336], P('rep', None, None, 'fsdp'), may hold values from -0.00059890747 to 0.00059890747
- v_gate_up: bfloat16 [4, 2, 2048, 14336], P('rep', None, None, 'fsdp'), may hold values from 9.968062e-10 to 9.9651515e-08
- m_down: bfloat16 [4, 14336, 2048], P('rep', 'fsdp'), may hold values from -0.00059890747 to 0.00059890747
- v_down: bfloat16 [4, 14336, 2048], P('rep', 'fsdp'), may hold values from 9.968062e-10 to 9.9651515e-08
Outputs:
- new_gate_up: float32 [2, 2048, 14336], P(None, 'rep', 'fsdp')
- new_down: float32 [14336, 2048], P('fsdp', 'rep')
- new_mom_gate_up: float32 [2, 2048, 14336], P(None, 'rep', 'fsdp')
- new_mom_down: float32 [14336, 2048], P('fsdp', 'rep')
The draws below stay inside these ranges and needn't reach their ends.
All inputs are finite; a program needn't handle non-finite values.
Results may differ from the reference program's by a relative error of at most 0.006.
Values may be sent and summed in bfloat16 or wider, within the bound.
A program may use at most 192 MiB of HBM per device.

```python
import math
import jax
import jax.numpy as jnp
from jax import lax

D = 2048
FF = 14336
TOK = 256
STEPS = 4
REPS = 4
ROWS = 256


def touch_ends(array, own_key, low, largest):
    longest = array.shape.index(max(array.shape))
    spots = []
    for shift in (0, 1):
        where = [jax.random.randint(jax.random.fold_in(own_key, axis), (), 0, length) for axis, length in enumerate(array.shape)]
        where[longest] = (where[longest] + shift) % array.shape[longest]
        spots.append(tuple(where))
    return array.at[spots[0]].set(low).at[spots[1]].set(largest)


def block_levels(key, extent, shards, smallest, top_value):
    gain, own = 1.0, jax.random.fold_in(key, 6)
    for dim, blocks in shards:
        steps = jnp.exp(jax.random.uniform(jax.random.fold_in(own, dim), (blocks,), jnp.float32, smallest / len(shards), top_value / len(shards)))
        gain = gain * jnp.repeat(steps, extent[dim] // blocks).reshape([-1 if axis == dim else 1 for axis in range(len(extent))])
    return gain


def bell_draw(rng, shape, deviation, bound, pieces=(), held_as=jnp.bfloat16):
    array = deviation * jax.random.normal(rng, shape, jnp.float32)
    if pieces:
        array = array * block_levels(rng, shape, pieces, -0.22, 0.18)
    return jnp.clip(array, -bound, bound).astype(held_as)


def setup_inputs(seed: int = 0) -> dict:
    arg_keys = jax.random.split(jax.random.key(seed), 13)
    in_table = bell_draw(arg_keys[0], (REPS, ROWS, D), 1.0, 6.0, ((0, 4),))
    target_table = bell_draw(arg_keys[1], (REPS, ROWS, D), 0.5, 3.0, ((0, 4),))
    in_ids = touch_ends(jax.random.randint(arg_keys[2], (REPS, STEPS, TOK), 0, ROWS), jax.random.fold_in(arg_keys[2], 1), 0, ROWS - 1).astype(jnp.int32)
    target_ids = touch_ends(jax.random.randint(arg_keys[3], (REPS, STEPS, TOK), 0, ROWS), jax.random.fold_in(arg_keys[3], 1), 0, ROWS - 1).astype(jnp.int32)
    gate_up = bell_draw(arg_keys[4], (2, D, FF), 1.0, 6.0, ((1, 4), (2, 32)), jnp.float32)
    down = bell_draw(arg_keys[5], (FF, D), 1.0, 6.0, ((0, 32), (1, 4)), jnp.float32)
    mom_gate_up = bell_draw(arg_keys[6], (2, D, FF), 0.1, 0.6, ((1, 4), (2, 32)), jnp.float32)
    mom_down = bell_draw(arg_keys[7], (FF, D), 0.1, 0.6, ((0, 32), (1, 4)), jnp.float32)
    m_gate_up = bell_draw(arg_keys[8], (REPS, 2, D, FF), 0.0001, 0.00059890747, ((0, 4), (3, 32)))
    v_gate_up = jnp.clip(jnp.exp(math.log(9.96515154838562e-08) - 4.604878 * jax.random.uniform(arg_keys[9], (REPS, 2, D, FF), jnp.float32) ** block_levels(arg_keys[9], (REPS, 2, D, FF), ((0, 4), (3, 32)), -0.2, 0.2)), 9.968061931431293e-10, 9.96515154838562e-08).astype(jnp.bfloat16)
    m_down = bell_draw(arg_keys[10], (REPS, FF, D), 0.0001, 0.00059890747, ((0, 4), (1, 32)))
    v_down = jnp.clip(jnp.exp(math.log(9.96515154838562e-08) - 4.604878 * jax.random.uniform(arg_keys[11], (REPS, FF, D), jnp.float32) ** block_levels(arg_keys[11], (REPS, FF, D), ((0, 4), (1, 32)), -0.2, 0.2)), 9.968061931431293e-10, 9.96515154838562e-08).astype(jnp.bfloat16)
    return dict(in_table=in_table, target_table=target_table, in_ids=in_ids, target_ids=target_ids, gate_up=gate_up, down=down, mom_gate_up=mom_gate_up, mom_down=mom_down, m_gate_up=m_gate_up, v_gate_up=v_gate_up, m_down=m_down, v_down=v_down)


beta_one = 0.9
beta_two = 0.95
inner_rate = 0.03
decay_rate = 0.1
epsilon = 1e-08
outer_rate = 0.7
momentum_rate = 0.9

def adam_update(weight, grad, first, second):
    first = beta_one * first + (1.0 - beta_one) * grad
    second = beta_two * second + (1.0 - beta_two) * grad * grad
    weight = weight - inner_rate * (first / (jnp.sqrt(second) + epsilon) + decay_rate * weight)
    return (weight, first, second)

def run_replica(table, targets, ids_in, ids_out, gate_up, down, first_gu, second_gu, first_down, second_down):
    in_scale = 1.0 / D ** 0.5
    out_scale = 1.0 / FF ** 0.5
    weight_gu = gate_up
    weight_down = down
    for step in range(STEPS):
        inputs = jnp.take(table, ids_in[step], axis=0)
        wanted = jnp.take(targets, ids_out[step], axis=0)
        gu_b = weight_gu.astype(jnp.bfloat16)
        down_b = weight_down.astype(jnp.bfloat16)
        gate = jnp.dot(inputs, gu_b[0], preferred_element_type=jnp.float32) * in_scale
        upper = jnp.dot(inputs, gu_b[1], preferred_element_type=jnp.float32) * in_scale
        hidden = (jax.nn.silu(gate) * upper).astype(jnp.bfloat16)
        output = jnp.dot(hidden, down_b, preferred_element_type=jnp.float32) * out_scale
        out_grad = ((output - wanted.astype(jnp.float32)) / TOK).astype(jnp.bfloat16)
        grad_down = jnp.dot(hidden.T, out_grad, preferred_element_type=jnp.float32) * out_scale
        hidden_grad = jnp.dot(out_grad, down_b.T, preferred_element_type=jnp.float32) * out_scale
        sigmoid_gate = jax.nn.sigmoid(gate)
        slope = sigmoid_gate * (1.0 + gate * (1.0 - sigmoid_gate))
        gate_grad = (hidden_grad * upper * slope).astype(jnp.bfloat16)
        up_grad = (hidden_grad * jax.nn.silu(gate)).astype(jnp.bfloat16)
        grad_gate = jnp.dot(inputs.T, gate_grad, preferred_element_type=jnp.float32) * in_scale
        grad_up = jnp.dot(inputs.T, up_grad, preferred_element_type=jnp.float32) * in_scale
        grad_gu = jnp.stack([grad_gate, grad_up])
        weight_gu, first_gu, second_gu = adam_update(weight_gu, grad_gu, first_gu, second_gu)
        weight_down, first_down, second_down = adam_update(weight_down, grad_down, first_down, second_down)
    return (weight_gu, weight_down)

def rounded(value):
    narrow = value.astype(jnp.bfloat16)
    narrow = lax.optimization_barrier(narrow)
    return narrow.astype(jnp.float32)

def reference(in_table, target_table, in_ids, target_ids, gate_up, down, mom_gate_up, mom_down, m_gate_up, v_gate_up, m_down, v_down):
    total_gu = jnp.zeros(gate_up.shape, jnp.float32)
    total_down = jnp.zeros(down.shape, jnp.float32)
    for replica in range(REPS):
        weight_gu, weight_down = run_replica(in_table[replica], target_table[replica], in_ids[replica], target_ids[replica], gate_up, down, m_gate_up[replica].astype(jnp.float32), v_gate_up[replica].astype(jnp.float32), m_down[replica].astype(jnp.float32), v_down[replica].astype(jnp.float32))
        total_gu = total_gu + rounded(gate_up - weight_gu)
        total_down = total_down + rounded(down - weight_down)
    delta_gu = total_gu / REPS
    delta_down = total_down / REPS
    new_mom_gu = momentum_rate * mom_gate_up + delta_gu
    new_mom_down = momentum_rate * mom_down + delta_down
    new_gu = gate_up - outer_rate * (delta_gu + momentum_rate * new_mom_gu)
    new_down = down - outer_rate * (delta_down + momentum_rate * new_mom_down)
    return (new_gu, new_down, new_mom_gu, new_mom_down)
```

```python
import functools
import math

import jax
import jax.numpy as jnp
from jax import lax
from jax.experimental import pallas as pl
from jax.experimental.pallas import tpu as pltpu
from jax.sharding import PartitionSpec as P

D = 2048
FF = 14336
STEPS = 4
TOK = 256
ROWS = 256
SHARDS = 32
HID = FF // SHARDS
SIDE = 4
BLOCKS = 4
BW = D // BLOCKS
BAND = TOK // SIDE
OWN = BAND // SIDE
HALF = BW // 2

beta_one = 0.9
beta_two = 0.95
inner_rate = 0.03
decay_rate = 0.1
epsilon = 1e-08
outer_rate = 0.7
momentum_rate = 0.9

in_scale = 1.0 / D**0.5
out_scale = 1.0 / FF**0.5
first_gain = inner_rate
step_gain = first_gain * (1.0 - beta_one)
second_gain = step_gain**2 / (1.0 - beta_two)
root_gain = math.sqrt(second_gain)
keep_rate = 1.0 - inner_rate * decay_rate

MESH = pl.DeviceIdType.MESH
VMEM = pltpu.VMEM
F32 = jnp.float32
BF16 = jnp.bfloat16


def adam(weight, grad, first, second, gain):
    t = grad * gain
    first = beta_one * first + t
    second = beta_two * second + t * t
    root = second * lax.rsqrt(second) + epsilon * root_gain
    move = first * pl.reciprocal(root, approx=True)
    return keep_rate * weight - root_gain * move, first, second


def inner_kernel(
    in_row_ids,
    in_col_ids,
    target_col_ids,
    table,
    table_t,
    targets,
    gu_hbm,
    down_hbm,
    m_gu_hbm,
    v_gu_hbm,
    m_down_hbm,
    v_down_hbm,
    p_gu_hbm,
    p_down_hbm,
    w_gu,
    m_gu,
    v_gu,
    b_gu,
    w_down,
    m_down,
    v_down,
    b_down,
    s_down,
    stage_gu,
    stage_down,
    inputs,
    inputs_t,
    pick,
    wanted,
    gate_buf,
    up_buf,
    slope_buf,
    silu_buf,
    hidden,
    hidden_t,
    hidden_grad,
    pre_grad,
    grad,
    partial,
    land_one,
    sum_one,
    land_two,
    out_grad,
    load_sem,
    gu_sem,
    down_sem,
    send_sem,
    recv_sem,
):
    rep = lax.axis_index("rep")
    fsdp = lax.axis_index("fsdp")
    zl = fsdp // (SIDE * SIDE)
    side = ((fsdp // SIDE) % SIDE, fsdp % SIDE)

    def peer(part, d_first, d_second, d_z):
        first = (side[part] + d_first) % SIDE
        second = (side[1 - part] + d_second) % SIDE
        z = (zl + d_z) % 2
        x, y = (first, second) if part == 0 else (second, first)
        return (rep, z * SIDE * SIDE + x * SIDE + y)

    cross = [(ds, dz) for ds in range(SIDE) for dz in range(2) if (ds, dz) != (0, 0)]
    partners = [peer(0, o, 0, dz) for o in range(1, SIDE) for dz in range(2)]
    partners += [peer(0, 0, ds, dz) for ds, dz in cross]

    barrier = pltpu.get_barrier_semaphore()
    for other in partners:
        pl.semaphore_signal(barrier, inc=1, device_id=other, device_id_type=MESH)

    load_gu = pltpu.make_async_copy(gu_hbm, b_gu, load_sem.at[0])
    load_down = pltpu.make_async_copy(down_hbm, b_down, load_sem.at[1])
    load_start = pltpu.make_async_copy(down_hbm, s_down, load_sem.at[2])
    load_gu.start()
    load_down.start()
    load_start.start()

    pieces = D // ROWS

    def gu_piece(i, slot):
        rows = pl.ds(pl.multiple_of((i % pieces) * ROWS, ROWS), ROWS)
        return [
            pltpu.make_async_copy(
                source.at[i // pieces, rows, :], stage_gu.at[slot, n], gu_sem.at[slot, n]
            )
            for n, source in enumerate((m_gu_hbm, v_gu_hbm))
        ]

    def down_piece(q, slot):
        return [
            pltpu.make_async_copy(
                source.at[:, pl.ds(q * BW, BW)], stage_down.at[slot, n], down_sem.at[slot, n]
            )
            for n, source in enumerate((m_down_hbm, v_down_hbm))
        ]

    for slot in range(2):
        for copy in gu_piece(slot, slot) + down_piece(slot, slot):
            copy.start()

    def load_gu_moments(i, carry):
        slot = i % 2
        for copy in gu_piece(i, slot):
            copy.wait()
        for r in range(0, ROWS, 64):
            rows = pl.ds(pl.multiple_of((i % pieces) * ROWS + r, 64), 64)
            m_gu[i // pieces, rows, :] = stage_gu[slot, 0, r : r + 64, :].astype(F32) * first_gain
            v_gu[i // pieces, rows, :] = stage_gu[slot, 1, r : r + 64, :].astype(F32) * second_gain

        @pl.when(i + 2 < 2 * pieces)
        def _():
            for copy in gu_piece(i + 2, slot):
                copy.start()

        return carry

    lax.fori_loop(0, 2 * pieces, load_gu_moments, 0)
    for q in range(BLOCKS):
        slot = q % 2
        for copy in down_piece(q, slot):
            copy.wait()
        cols = pl.ds(q * BW, BW)

        def load_down_moments(i, carry):
            rows = pl.ds(pl.multiple_of(i * 64, 64), 64)
            m_down[rows, cols] = stage_down[slot, 0, rows, :].astype(F32) * first_gain
            v_down[rows, cols] = stage_down[slot, 1, rows, :].astype(F32) * second_gain
            return carry

        lax.fori_loop(0, HID // 64, load_down_moments, 0)
        if q + 2 < BLOCKS:
            for copy in down_piece(q + 2, slot):
                copy.start()

    load_gu.wait()
    load_down.wait()
    load_start.wait()

    def widen_gu(i, carry):
        rows = pl.ds(pl.multiple_of((i % 32) * 64, 64), 64)
        w_gu[i // 32, rows, :] = b_gu[i // 32, rows, :].astype(F32)
        return carry

    lax.fori_loop(0, 64, widen_gu, 0)

    def widen_down(i, carry):
        rows = pl.ds(pl.multiple_of(i * 16, 16), 16)
        w_down[rows, :] = b_down[rows, :].astype(F32)
        return carry

    lax.fori_loop(0, HID // 16, widen_down, 0)

    def look_up_inputs(k):
        rows = lax.broadcasted_iota(jnp.int32, (TOK, ROWS), 1)
        chosen = (in_col_ids[k] == rows).astype(F32).astype(BF16)
        inputs[...] = jnp.dot(chosen, table[...], preferred_element_type=F32).astype(BF16)

    look_up_inputs(0)
    pl.semaphore_wait(barrier, len(partners))

    def band(coordinate):
        return pl.ds(pl.multiple_of(coordinate * BAND, BAND), BAND)

    def own_rows(first, second):
        return pl.ds(pl.multiple_of(first * BAND + second * OWN, OWN), OWN)

    def own_cols(z):
        return pl.ds(pl.multiple_of(z * HALF, HALF), HALF)

    def send(kind, q, src, dst, other):
        pltpu.make_async_remote_copy(
            src_ref=src,
            dst_ref=dst,
            send_sem=send_sem.at[kind, q],
            recv_sem=recv_sem.at[kind, q],
            device_id=other,
            device_id_type=MESH,
        ).start()

    def wait_bytes(kind, q, sem):
        like = land_one.at[q] if kind in (0, 3) else land_two.at[q]
        pltpu.make_async_copy(like, like, sem.at[kind, q]).wait()

    def scatter_one(q):
        part = q % 2
        for o in range(1, SIDE):
            to = (side[part] + o) % SIDE
            send(0, q, partial.at[q, band(to), :], land_one.at[q, o - 1], peer(part, o, 0, 0))

    def scatter_two(q):
        part = q % 2
        wait_bytes(0, q, recv_sem)
        total = partial[q, band(side[part]), :].astype(F32)
        for o in range(SIDE - 1):
            total = total + land_one[q, o].astype(F32)
        sum_one[q] = total.astype(BF16)
        for n, (ds, dz) in enumerate(cross):
            to = (side[1 - part] + ds) % SIDE
            rows = pl.ds(pl.multiple_of(to * OWN, OWN), OWN)
            src = sum_one.at[q, rows, own_cols((zl + dz) % 2)]
            send(1, q, src, land_two.at[q, n], peer(part, 0, ds, dz))

    def gather_one(q):
        part = q % 2
        wait_bytes(1, q, recv_sem)
        rows = pl.ds(pl.multiple_of(side[1 - part] * OWN, OWN), OWN)
        total = sum_one[q, rows, own_cols(zl)].astype(F32)
        for n in range(len(cross)):
            total = total + land_two[q, n].astype(F32)
        mine = (q, own_rows(side[part], side[1 - part]), own_cols(zl))
        out_grad[mine] = ((total - wanted[q]) * (1.0 / TOK)).astype(BF16)
        for ds, dz in cross:
            send(2, q, out_grad.at[mine], out_grad.at[mine], peer(part, 0, ds, dz))

    def gather_two(q):
        part = q % 2
        wait_bytes(2, q, recv_sem)
        mine = out_grad.at[q, band(side[part]), :]
        for o in range(1, SIDE):
            send(3, q, mine, mine, peer(part, o, 0, 0))

    def update_down(q, last):
        cols = pl.ds(q * BW, BW)

        def rows_of(i, carry):
            rows = pl.ds(pl.multiple_of(i * 16, 16), 16)
            weight, first, second = adam(
                w_down[rows, cols],
                grad[rows, :],
                m_down[rows, cols],
                v_down[rows, cols],
                step_gain * out_scale,
            )
            if last:
                b_down[rows, cols] = (s_down[rows, cols].astype(F32) - weight).astype(BF16)
            else:
                w_down[rows, cols] = weight
                m_down[rows, cols] = first
                v_down[rows, cols] = second
                b_down[rows, cols] = weight.astype(BF16)
            return carry

        lax.fori_loop(0, HID // 16, rows_of, 0, unroll=2)

    def update_gu(j, base, last):
        def rows_of(i, carry):
            here = pl.ds(pl.multiple_of(i * 16, 16), 16)
            rows = pl.ds(pl.multiple_of(base + i * 16, 16), 16)
            weight, first, second = adam(
                w_gu[j, rows, :],
                grad[here, :HID],
                m_gu[j, rows, :],
                v_gu[j, rows, :],
                step_gain * in_scale,
            )
            if last:
                b_gu[j, rows, :] = (b_gu[j, rows, :].astype(F32) - weight).astype(BF16)
            else:
                w_gu[j, rows, :] = weight
                m_gu[j, rows, :] = first
                v_gu[j, rows, :] = second
                b_gu[j, rows, :] = weight.astype(BF16)
            return carry

        lax.fori_loop(0, ROWS // 16, rows_of, 0, unroll=2)

    def use_block(q, k):
        wait_bytes(3, q, recv_sem)
        cols = pl.ds(q * BW, BW)
        product = lax.dot_general(
            out_grad[q], b_down[:, cols], (((1,), (1,)), ((), ())), preferred_element_type=F32
        )
        if q == 0:
            hidden_grad[...] = product
        else:
            hidden_grad[...] += product
        grad[:HID, :] = jnp.dot(hidden_t[...], out_grad[q], preferred_element_type=F32)

        @pl.when(k < STEPS - 1)
        def _():
            update_down(q, False)

        @pl.when(k == STEPS - 1)
        def _():
            update_down(q, True)

    def step(k, carry):
        gate_buf[...] = jnp.dot(inputs[...], b_gu[0], preferred_element_type=F32)
        up_buf[...] = jnp.dot(inputs[...], b_gu[1], preferred_element_type=F32)

        @pl.when(k == STEPS - 1)
        def _():
            load_gu.start()

        def activate(i, carry):
            rows = pl.ds(pl.multiple_of(i * 32, 32), 32)
            gate = gate_buf[rows, :] * in_scale
            upper = up_buf[rows, :] * in_scale
            sigmoid = jax.nn.sigmoid(gate)
            silu = gate * sigmoid
            hidden[rows, :] = (silu * upper).astype(BF16)
            silu_buf[rows, :] = silu * out_scale
            slope_buf[rows, :] = upper * sigmoid * (1.0 + gate * (1.0 - sigmoid)) * out_scale
            return carry

        lax.fori_loop(0, TOK // 32, activate, 0)

        for q in range(BLOCKS):
            cols = pl.ds(q * BW, BW)
            product = jnp.dot(hidden[...], b_down[:, cols], preferred_element_type=F32)
            partial[q] = (product * out_scale).astype(BF16)
            scatter_one(q)

        hidden_t[...] = hidden[...].T
        rows = lax.broadcasted_iota(jnp.int32, (TOK, ROWS), 1)
        pick[...] = (target_col_ids[k] == rows).astype(F32).astype(BF16)
        for q in range(BLOCKS):
            part = q % 2
            chosen = pick[own_rows(side[part], side[1 - part]), :]
            cols = pl.ds(pl.multiple_of(q * BW + zl * HALF, HALF), HALF)
            wanted[q] = jnp.dot(chosen, targets[:, cols], preferred_element_type=F32)
        tall = lax.broadcasted_iota(jnp.int32, (ROWS, TOK), 0)
        chosen_t = (in_row_ids[k] == tall).astype(F32).astype(BF16)
        inputs_t[...] = jnp.dot(table_t[...], chosen_t, preferred_element_type=F32).astype(BF16)
        look_up_inputs(jnp.minimum(k + 1, STEPS - 1))

        scatter_two(0)
        scatter_two(1)
        gather_one(0)
        scatter_two(2)
        gather_one(1)
        scatter_two(3)
        gather_two(0)
        gather_one(2)
        gather_two(1)
        gather_one(3)
        gather_two(2)
        use_block(0, k)
        gather_two(3)
        use_block(1, k)
        use_block(2, k)
        use_block(3, k)

        pre_grad[0] = (hidden_grad[...] * slope_buf[...]).astype(BF16)
        pre_grad[1] = (hidden_grad[...] * silu_buf[...]).astype(BF16)

        @pl.when(k == STEPS - 1)
        def _():
            load_gu.wait()

        def update_piece(i, carry):
            base = pl.multiple_of(i * ROWS, ROWS)
            for j in range(2):
                grad[:ROWS, :HID] = jnp.dot(
                    inputs_t[pl.ds(base, ROWS), :], pre_grad[j], preferred_element_type=F32
                )

                @pl.when(k < STEPS - 1)
                def _():
                    update_gu(j, base, False)

                @pl.when(k == STEPS - 1)
                def _():
                    update_gu(j, base, True)

            return carry

        lax.fori_loop(0, D // ROWS, update_piece, 0)

        for q in range(BLOCKS):
            for kind in range(4):
                wait_bytes(kind, q, send_sem)
        return carry

    lax.fori_loop(0, STEPS, step, 0)

    store_gu = pltpu.make_async_copy(b_gu, p_gu_hbm, load_sem.at[0])
    store_down = pltpu.make_async_copy(b_down, p_down_hbm, load_sem.at[1])
    store_gu.start()
    store_down.start()
    store_gu.wait()
    store_down.wait()


def inner_steps(in_ids, target_ids, table, targets, gu, down, m_gu, v_gu, m_down, v_down):
    in_vmem = pl.BlockSpec(memory_space=VMEM)
    anywhere = pl.BlockSpec(memory_space=pl.ANY)
    gu_shape, down_shape = (2, D, HID), (HID, D)
    return pl.pallas_call(
        inner_kernel,
        out_shape=(
            jax.ShapeDtypeStruct(gu_shape, BF16),
            jax.ShapeDtypeStruct(down_shape, BF16),
        ),
        in_specs=[in_vmem] * 6 + [anywhere] * 6,
        out_specs=(anywhere, anywhere),
        scratch_shapes=[
            VMEM(gu_shape, F32),
            VMEM(gu_shape, F32),
            VMEM(gu_shape, F32),
            VMEM(gu_shape, BF16),
            VMEM(down_shape, F32),
            VMEM(down_shape, F32),
            VMEM(down_shape, F32),
            VMEM(down_shape, BF16),
            VMEM(down_shape, BF16),
            VMEM((2, 2, ROWS, HID), BF16),
            VMEM((2, 2, HID, BW), BF16),
            VMEM((TOK, D), BF16),
            VMEM((D, TOK), BF16),
            VMEM((TOK, ROWS), BF16),
            VMEM((BLOCKS, OWN, HALF), F32),
            VMEM((TOK, HID), F32),
            VMEM((TOK, HID), F32),
            VMEM((TOK, HID), F32),
            VMEM((TOK, HID), F32),
            VMEM((TOK, HID), BF16),
            VMEM((HID, TOK), BF16),
            VMEM((TOK, HID), F32),
            VMEM((2, TOK, HID), BF16),
            VMEM((HID, BW), F32),
            VMEM((BLOCKS, TOK, BW), BF16),
            VMEM((BLOCKS, SIDE - 1, BAND, BW), BF16),
            VMEM((BLOCKS, BAND, BW), BF16),
            VMEM((BLOCKS, 2 * SIDE - 1, OWN, HALF), BF16),
            VMEM((BLOCKS, TOK, BW), BF16),
            pltpu.SemaphoreType.DMA((3,)),
            pltpu.SemaphoreType.DMA((2, 2)),
            pltpu.SemaphoreType.DMA((2, 2)),
            pltpu.SemaphoreType.DMA((4, BLOCKS)),
            pltpu.SemaphoreType.DMA((4, BLOCKS)),
        ],
        compiler_params=pltpu.CompilerParams(
            collective_id=0, has_side_effects=True, vmem_limit_bytes=60 * 2**20
        ),
        name="inner_steps",
    )(
        in_ids[:, None, :],
        in_ids[:, :, None],
        target_ids[:, :, None],
        table,
        table.T,
        targets,
        gu,
        down,
        m_gu,
        v_gu,
        m_down,
        v_down,
    )


def on_device(
    in_table,
    target_table,
    in_ids,
    target_ids,
    gate_up,
    down,
    mom_gate_up,
    mom_down,
    m_gate_up,
    v_gate_up,
    m_down,
    v_down,
):
    start_gu = lax.all_gather(gate_up.astype(BF16), "rep", axis=1, tiled=True)
    start_down = lax.all_gather(down.astype(BF16), "rep", axis=1, tiled=True)
    delta_gu, delta_down = inner_steps(
        in_ids[0],
        target_ids[0],
        in_table[0],
        target_table[0],
        start_gu,
        start_down,
        m_gate_up[0],
        v_gate_up[0],
        m_down[0],
        v_down[0],
    )
    total_gu = lax.psum_scatter(delta_gu, "rep", scatter_dimension=1, tiled=True).astype(F32)
    total_down = lax.psum_scatter(delta_down, "rep", scatter_dimension=1, tiled=True).astype(F32)
    replicas = lax.axis_size("rep")
    mean_gu = total_gu / replicas
    mean_down = total_down / replicas
    new_mom_gu = momentum_rate * mom_gate_up + mean_gu
    new_mom_down = momentum_rate * mom_down + mean_down
    new_gu = gate_up - outer_rate * (mean_gu + momentum_rate * new_mom_gu)
    new_down = down - outer_rate * (mean_down + momentum_rate * new_mom_down)
    return (new_gu, new_down, new_mom_gu, new_mom_down)


def solution(mesh):
    in_specs = (
        P("rep", None, None),
        P("rep", None, None),
        P("rep", None, None),
        P("rep", None, None),
        P(None, "rep", "fsdp"),
        P("fsdp", "rep"),
        P(None, "rep", "fsdp"),
        P("fsdp", "rep"),
        P("rep", None, None, "fsdp"),
        P("rep", None, None, "fsdp"),
        P("rep", "fsdp", None),
        P("rep", "fsdp", None),
    )
    out_specs = (P(None, "rep", "fsdp"), P("fsdp", "rep"), P(None, "rep", "fsdp"), P("fsdp", "rep"))
    return jax.shard_map(
        on_device, mesh=mesh, in_specs=in_specs, out_specs=out_specs, check_vma=False
    )
```

```python
import math

import jax
import jax.numpy as jnp
from jax import lax
from jax.experimental import pallas as pl
from jax.experimental.pallas import tpu as pltpu
from jax.sharding import PartitionSpec as P

D = 2048
FF = 14336
STEPS = 4
TOK = 256
ROWS = 256
SHARDS = 32
HID = FF // SHARDS
SIDE = 4
REPS = 4
BW = D // REPS
BAND = TOK // SIDE
OWN = BAND // SIDE
HALF = BW // 2
THIN = HALF // 2
CUTS = 4
CUT = HID // CUTS
IN_FLIGHT = 3

beta_one = 0.9
beta_two = 0.95
inner_rate = 0.03
decay_rate = 0.1
epsilon = 1e-08
outer_rate = 0.7
momentum_rate = 0.9

in_scale = 1.0 / D**0.5
out_scale = 1.0 / FF**0.5
first_gain = inner_rate
step_gain = first_gain * (1.0 - beta_one)
second_gain = step_gain**2 / (1.0 - beta_two)
root_gain = math.sqrt(second_gain)
keep_rate = 1.0 - inner_rate * decay_rate

MESH = pl.DeviceIdType.MESH
VMEM = pltpu.VMEM
F32 = jnp.float32
BF16 = jnp.bfloat16


def adam(weight, grad, first, second, gain):
    t = grad * gain
    first = beta_one * first + t
    second = beta_two * second + t * t
    root = second * lax.rsqrt(second) + epsilon * root_gain
    move = first * pl.reciprocal(root, approx=True)
    return keep_rate * weight - root_gain * move, first, second


def dot(a, b):
    return jnp.dot(a, b, preferred_element_type=F32)


def dot_last(a, b):
    return lax.dot_general(a, b, (((1,), (1,)), ((), ())), preferred_element_type=F32)


def round_kernel(
    in_ids,
    target_ids,
    table_hbm,
    targets_hbm,
    outer_gu,
    outer_down,
    m_gu,
    v_gu,
    m_down,
    v_down,
    mom_gu,
    mom_down,
    new_gu,
    new_down,
    new_mom_gu,
    new_mom_down,
    table,
    targets,
    weight,
    first,
    second,
    start,
    narrow,
    stage,
    inputs,
    pick,
    wanted,
    gate_up_buf,
    slope_buf,
    silu_buf,
    hidden_grad,
    hidden_t,
    hidden,
    pre_grad,
    partial,
    land_one,
    sum_one,
    land_two,
    out_grad,
    land_mate,
    land_far,
    table_sem,
    load_sem,
    stage_sem,
    send_sem,
    recv_sem,
    z_send,
    z_recv,
    core_send,
    core_recv,
    fwd_send,
    fwd_recv,
    mate_send,
    mate_recv,
    far_send,
    far_recv,
    outer_sem,
    out_sem,
):
    rep = lax.axis_index("rep")
    fsdp = lax.axis_index("fsdp")
    zh, core = rep // 2, rep % 2
    zl = fsdp // (SIDE * SIDE)
    side = ((fsdp // SIDE) % SIDE, fsdp % SIDE)
    mate = (zh * 2 + (1 - core), fsdp)
    far = ((1 - zh) * 2 + core, fsdp)

    def quarter(n):
        return ((zh + n // 2) % 2) * 2 + (core + n % 2) % 2

    def cols_of(n):
        return pl.ds(pl.multiple_of(quarter(n) * BW, BW), BW)

    def peer(part, d_first, d_second, d_z):
        one = (side[part] + d_first) % SIDE
        two = (side[1 - part] + d_second) % SIDE
        z = (zl + d_z) % 2
        x, y = (one, two) if part == 0 else (two, one)
        return (rep, z * SIDE * SIDE + x * SIDE + y)

    cross = [(2, 1), (1, 1), (3, 1), (2, 0), (1, 0), (3, 0), (0, 1)]
    along = (2, 1, 3)
    partners = [mate, far]
    partners += [peer(0, o, 0, dz) for o in range(1, SIDE) for dz in range(2)]
    partners += [peer(0, 0, ds, dz) for ds, dz in cross]

    barrier = pltpu.get_barrier_semaphore()
    for other in partners:
        pl.semaphore_signal(barrier, inc=1, device_id=other, device_id_type=MESH)

    def in_rows(count, height, body, unroll=1):
        def go(i, carry):
            body(pl.ds(pl.multiple_of(i * height, height), height))
            return carry

        lax.fori_loop(0, count // height, go, 0, unroll=unroll)

    def remote(src, dst, one, two, other):
        return pltpu.make_async_remote_copy(
            src_ref=src,
            dst_ref=dst,
            send_sem=one,
            recv_sem=two,
            device_id=other,
            device_id_type=MESH,
        )

    def outer_cut(j, c):
        rows = pl.ds(c * CUT, CUT)
        source = outer_gu.at[j] if j < 2 else outer_down
        return pltpu.make_async_copy(
            source.at[rows, :], weight.at[0, j, rows, :], load_sem.at[j, c]
        )

    for j in range(3):
        for c in range(CUTS):
            outer_cut(j, c).start()
    tables = [
        pltpu.make_async_copy(source, held, table_sem.at[i])
        for i, (source, held) in enumerate(((table_hbm, table), (targets_hbm, targets)))
    ]
    for copy in tables:
        copy.start()
    blocks = [(j, n) for j in range(3) for n in range(REPS)]

    def moment_copies(i):
        j, n = blocks[i]
        sources = (m_gu.at[j], v_gu.at[j]) if j < 2 else (m_down, v_down)
        return [
            pltpu.make_async_copy(
                source.at[:, cols_of(n)], stage.at[i % 2, s], stage_sem.at[i % 2, s]
            )
            for s, source in enumerate(sources)
        ]

    for i in range(2):
        for copy in moment_copies(i):
            copy.start()

    def narrow_outer(j, c):
        outer_cut(j, c).wait()
        for r in range(0, CUT, 16):
            rows = pl.ds(c * CUT + r, 16)
            start[0, j, rows, :] = weight[0, j, rows, :].astype(BF16)

    narrow_outer(0, 0)
    pl.semaphore_wait(barrier, len(partners))

    cuts = [(j, c) for j in range(3) for c in range(CUTS)]

    def z_copy(i):
        j, c = cuts[i]
        rows = pl.ds(c * CUT, CUT)
        return remote(
            start.at[0, j, rows, :], start.at[2, j, rows, :], z_send.at[i], z_recv.at[i], far
        )

    def fwd_copy(i):
        j, c = cuts[i]
        rows = pl.ds(c * CUT, CUT)
        return remote(
            start.at[2, j, rows, :], start.at[3, j, rows, :], fwd_send.at[i], fwd_recv.at[i], mate
        )

    def core_copy(j):
        return remote(start.at[0, j], start.at[1, j], core_send.at[j], core_recv.at[j], mate)

    for j, c in cuts:
        if (j, c) != (0, 0):
            narrow_outer(j, c)
        if j * CUTS + c < IN_FLIGHT:
            z_copy(j * CUTS + c).start()
        if c == CUTS - 1:
            core_copy(j).start()

    def widen(j, n):
        def rows_of(rows):
            weight[n, j, rows, :] = start[n, j, rows, :].astype(F32)

        in_rows(HID, 16, rows_of, 2)

    def take_moments(i):
        j, n = blocks[i]
        for copy in moment_copies(i):
            copy.wait()

        def rows_of(rows):
            first[n, j, rows, :] = stage[i % 2, 0, rows, :].astype(F32) * first_gain
            second[n, j, rows, :] = stage[i % 2, 1, rows, :].astype(F32) * second_gain

        in_rows(HID, 16, rows_of, 2)
        if i + 2 < len(blocks):
            for copy in moment_copies(i + 2):
                copy.start()

    def take_cut(i):
        copy = z_copy(i)
        copy.wait_recv()
        fwd_copy(i).start()
        copy.wait_send()
        if i + IN_FLIGHT < len(cuts):
            z_copy(i + IN_FLIGHT).start()

    def chosen_t(ids, k):
        rows = lax.broadcasted_iota(jnp.int32, (ROWS, TOK), 0)
        return (ids[pl.ds(k, 1), :] == rows).astype(F32)

    def look_up_inputs(k, slot):
        chosen = chosen_t(in_ids, k).T.astype(BF16)
        for n in range(REPS):
            inputs[slot, n] = dot(chosen, table[:, cols_of(n)]).astype(BF16)

    def band(coordinate):
        return pl.ds(pl.multiple_of(coordinate * BAND, BAND), BAND)

    def own_rows(one, two):
        return pl.ds(pl.multiple_of(one * BAND + two * OWN, OWN), OWN)

    def thin_cols(base, z):
        return pl.ds(pl.multiple_of(base + z * THIN, THIN), THIN)

    def send(kind, n, h, src, dst, other):
        remote(src, dst, send_sem.at[kind, n, h], recv_sem.at[kind, n, h], other).start()

    def wait_bytes(kind, n, h, sem):
        like = land_one.at[n, h] if kind in (0, 3) else land_two.at[n, h]
        pltpu.make_async_copy(like, like, sem.at[kind, n, h]).wait()

    def scatter_one(n, held):
        partial[n] = (dot(hidden[...], held[n, 2]) * out_scale).astype(BF16)
        for h in range(2):
            cols = pl.ds(h * HALF, HALF)
            for o in along:
                src = partial.at[n, band((side[h] + o) % SIDE), cols]
                send(0, n, h, src, land_one.at[n, h, o - 1], peer(h, o, 0, 0))

    def scatter_two(n):
        for h in range(2):
            wait_bytes(0, n, h, recv_sem)
            total = partial[n, band(side[h]), pl.ds(h * HALF, HALF)].astype(F32)
            for o in range(SIDE - 1):
                total = total + land_one[n, h, o].astype(F32)
            sum_one[n, h] = total.astype(BF16)
            for i, (ds, dz) in enumerate(cross):
                to = (side[1 - h] + ds) % SIDE
                rows = pl.ds(pl.multiple_of(to * OWN, OWN), OWN)
                src = sum_one.at[n, h, rows, thin_cols(0, (zl + dz) % 2)]
                send(1, n, h, src, land_two.at[n, h, i], peer(h, 0, ds, dz))

    def gather_one(n):
        for h in range(2):
            wait_bytes(1, n, h, recv_sem)
            rows = pl.ds(pl.multiple_of(side[1 - h] * OWN, OWN), OWN)
            total = sum_one[n, h, rows, thin_cols(0, zl)].astype(F32)
            for i in range(len(cross)):
                total = total + land_two[n, h, i].astype(F32)
            mine = (n, own_rows(side[h], side[1 - h]), thin_cols(h * HALF, zl))
            out_grad[mine] = ((total - wanted[n, h]) * (1.0 / TOK)).astype(BF16)
            for ds, dz in cross:
                send(2, n, h, out_grad.at[mine], out_grad.at[mine], peer(h, 0, ds, dz))

    def gather_two(n):
        for h in range(2):
            wait_bytes(2, n, h, recv_sem)
            mine = out_grad.at[n, band(side[h]), pl.ds(h * HALF, HALF)]
            for o in along:
                send(3, n, h, mine, mine, peer(h, o, 0, 0))

    def update(n, j, product, last):
        gain = step_gain * (in_scale if j < 2 else out_scale)
        for r in range(0, HID, 16):
            here = (n, j, pl.ds(r, 16), slice(None))
            w, m, v = adam(weight[here], product[r : r + 16, :], first[here], second[here], gain)
            if last:
                narrow[here] = (start[here].astype(F32) - w).astype(BF16)
            else:
                weight[here] = w
                first[here] = m
                second[here] = v
                narrow[here] = w.astype(BF16)

    def use_block(n, held, fresh):
        for h in range(2):
            wait_bytes(3, n, h, recv_sem)
        product = dot_last(held[n, 2], out_grad[n])
        if fresh:
            hidden_grad[...] = product
        else:
            hidden_grad[...] += product

    def update_down(n, slot, last):
        update(n, 2, dot(hidden_t[slot], out_grad[n]), last)

    def update_gu(n, slot, last):
        product = dot(pre_grad[...], inputs[slot, n])
        for j in range(2):
            update(n, j, product[j * HID : (j + 1) * HID, :], last)

    def update_all_gu(slot):
        for n in range(REPS):
            update_gu(n, slot, False)

    def update_late(slot):
        for n in range(2):
            update_down(n, slot, False)

    def forward(held, slot):
        both = [held[n, 0:2].reshape(2 * HID, BW) for n in range(REPS)]
        rows_in = jnp.concatenate([inputs[slot, n] for n in range(REPS)], axis=1)
        gate_up_buf[...] = dot_last(jnp.concatenate(both, axis=1), rows_in)
        for r in range(0, HID, 16):
            rows = pl.ds(r, 16)
            gate = gate_up_buf[rows, :] * in_scale
            upper = gate_up_buf[pl.ds(HID + r, 16), :] * in_scale
            sigmoid = jax.nn.sigmoid(gate)
            silu = gate * sigmoid
            hidden_t[slot, rows, :] = (silu * upper).astype(BF16)
            silu_buf[rows, :] = silu * out_scale
            slope_buf[rows, :] = upper * sigmoid * (1.0 + gate * (1.0 - sigmoid)) * out_scale
        hidden[...] = hidden_t[slot].T

    def look_up_targets(k):
        pick[...] = chosen_t(target_ids, k).T.astype(BF16)
        for n in range(REPS):
            for h in range(2):
                rows = own_rows(side[h], side[1 - h])
                cols = thin_cols(quarter(n) * BW + h * HALF, zl)
                wanted[n, h] = dot(pick[rows, :], targets[:, cols])

    def backward():
        pre_grad[:HID, :] = (hidden_grad[...] * slope_buf[...]).astype(BF16)
        pre_grad[HID:, :] = (hidden_grad[...] * silu_buf[...]).astype(BF16)

    def end_sends():
        for n in range(REPS):
            for kind in range(4):
                for h in range(2):
                    wait_bytes(kind, n, h, send_sem)

    for copy in tables:
        copy.wait()
    look_up_inputs(0, 0)
    for j in range(3):
        widen(j, 0)
    for i in range(2 * CUTS):
        take_moments(i)
        take_cut(i)
    for j in range(2):
        core_copy(j).wait_recv()
        widen(j, 1)
    for i in range(2 * CUTS):
        fwd_copy(i).wait_recv()
    forward(start, 0)
    core_copy(2).wait_recv()
    scatter_one(0, start)
    scatter_one(1, start)
    look_up_targets(0)
    take_cut(8)
    take_moments(8)
    scatter_two(0)
    scatter_two(1)
    take_cut(9)
    widen(2, 1)
    gather_one(0)
    gather_one(1)
    take_cut(10)
    take_moments(9)
    gather_two(0)
    gather_two(1)
    take_cut(11)
    for i in range(2 * CUTS, 3 * CUTS):
        fwd_copy(i).wait_recv()
    scatter_one(2, start)
    scatter_one(3, start)
    take_moments(10)
    take_moments(11)
    use_block(0, start, True)
    scatter_two(2)
    scatter_two(3)
    use_block(1, start, False)
    look_up_inputs(1, 1)
    gather_one(2)
    gather_one(3)
    for j in range(3):
        widen(j, 2)
        widen(j, 3)
    gather_two(2)
    gather_two(3)
    for n in (2, 3):
        use_block(n, start, False)
        update_down(n, 0, False)
    backward()
    update_all_gu(0)
    end_sends()

    def middle(k, slot, order, last):
        a, b, c, d = order
        forward(narrow, slot)
        scatter_one(a, narrow)
        scatter_one(b, narrow)
        update_late(1 - slot)
        if last:
            look_up_targets(k)
            for n in (a, b):
                scatter_two(n)
            for n in (c, d):
                scatter_one(n, narrow)
            for n in (a, b):
                gather_one(n)
            for n in (c, d):
                scatter_two(n)
            for n in (a, b):
                gather_two(n)
            for n in (c, d):
                gather_one(n)
            use_block(a, narrow, True)
            update_down(a, slot, True)
            return
        scatter_one(c, narrow)
        scatter_one(d, narrow)
        look_up_targets(k)
        look_up_inputs(k + 1, 1 - slot)
        for stage_of in (scatter_two, gather_one, gather_two):
            for n in order:
                stage_of(n)
        use_block(a, narrow, True)
        update_down(a, slot, False)

    def step(k, carry):
        slot = k % 2
        middle(k, slot, (2, 3, 0, 1), False)
        use_block(3, narrow, False)
        update_down(3, slot, False)
        use_block(0, narrow, False)
        use_block(1, narrow, False)
        backward()
        update_all_gu(slot)
        end_sends()
        return carry

    lax.fori_loop(1, STEPS - 1, step, 0)

    def mate_copy(j, n):
        return remote(
            narrow.at[n, j],
            land_mate.at[j, n // 2],
            mate_send.at[j, n // 2],
            mate_recv.at[j, n // 2],
            mate,
        )

    def far_copy(j, c):
        rows = pl.ds(c * CUT, CUT)
        return remote(
            narrow.at[2, j, rows, :], land_far.at[j, rows, :], far_send.at[j, c], far_recv.at[j, c], far
        )

    def pair_sum(j):
        mate_copy(j, 3).wait_recv()
        for c in range(CUTS):
            def rows_of(r):
                rows = pl.ds(pl.multiple_of(c * CUT + r * 16, 16), 16)
                both = narrow[2, j, rows, :].astype(F32) + land_mate[j, 1, rows, :].astype(F32)
                narrow[2, j, rows, :] = both.astype(BF16)

            for r in range(CUT // 16):
                rows_of(r)
            far_copy(j, c).start()

    outer_loads = [
        pltpu.make_async_copy(source.at[j] if j < 2 else flat, held.at[3, j], outer_sem.at[i, j])
        for i, (source, flat, held) in enumerate(
            ((outer_gu, outer_down, first), (mom_gu, mom_down, second))
        )
        for j in range(3)
    ]
    slot = (STEPS - 1) % 2
    middle(STEPS - 1, slot, (3, 2, 0, 1), True)
    mate_copy(2, 3).start()
    use_block(2, narrow, False)
    update_down(2, slot, True)
    gather_two(0)
    gather_two(1)
    pair_sum(2)
    use_block(0, narrow, False)
    use_block(1, narrow, False)
    backward()
    update_gu(3, slot, True)
    for j in range(2):
        mate_copy(j, 3).start()
    for copy in outer_loads:
        copy.start()
    update_gu(2, slot, True)
    for j in range(2):
        pair_sum(j)
    update_down(1, slot, True)
    mate_copy(2, 1).start()
    update_gu(1, slot, True)
    for j in range(2):
        mate_copy(j, 1).start()
    update_down(0, slot, True)
    update_gu(0, slot, True)
    end_sends()

    def out_copies(j, c):
        rows = pl.ds(c * CUT, CUT)
        outs = (new_gu.at[j], new_mom_gu.at[j]) if j < 2 else (new_down, new_mom_down)
        return [
            pltpu.make_async_copy(
                weight.at[i, j, rows, :], out.at[rows, :], out_sem.at[j, c, i]
            )
            for i, out in enumerate(outs)
        ]

    for copy in outer_loads:
        copy.wait()
    for j in (2, 0, 1):
        mate_copy(j, 1).wait_recv()
        for c in range(CUTS):
            far_copy(j, c).wait_recv()
            for r in range(CUT // 16):
                rows = pl.ds(c * CUT + r * 16, 16)
                total = (
                    narrow[0, j, rows, :].astype(F32)
                    + land_mate[j, 0, rows, :].astype(F32)
                    + land_far[j, rows, :].astype(F32)
                )
                mean = total / REPS
                new_mom = momentum_rate * second[3, j, rows, :] + mean
                weight[1, j, rows, :] = new_mom
                weight[0, j, rows, :] = first[3, j, rows, :] - outer_rate * (
                    mean + momentum_rate * new_mom
                )
            for copy in out_copies(j, c):
                copy.start()

    for j in range(3):
        core_copy(j).wait_send()
        for n in (1, 3):
            mate_copy(j, n).wait_send()
        for c in range(CUTS):
            far_copy(j, c).wait_send()
            for copy in out_copies(j, c):
                copy.wait()
    for i in range(len(cuts)):
        fwd_copy(i).wait_send()


def whole_round(in_ids, target_ids, table, targets, outer_gu, outer_down, *moments):
    in_vmem = pl.BlockSpec(memory_space=VMEM)
    anywhere = pl.BlockSpec(memory_space=pl.ANY)
    every = (REPS, 3, HID, BW)
    dma = pltpu.SemaphoreType.DMA
    gu_shape = jax.ShapeDtypeStruct((2, HID, BW), F32)
    down_shape = jax.ShapeDtypeStruct((HID, BW), F32)
    return pl.pallas_call(
        round_kernel,
        out_shape=(gu_shape, down_shape, gu_shape, down_shape),
        in_specs=[in_vmem] * 2 + [anywhere] * 10,
        out_specs=(anywhere,) * 4,
        scratch_shapes=[
            VMEM((ROWS, D), BF16),
            VMEM((ROWS, D), BF16),
            VMEM(every, F32),
            VMEM(every, F32),
            VMEM(every, F32),
            VMEM(every, BF16),
            VMEM(every, BF16),
            VMEM((2, 2, HID, BW), BF16),
            VMEM((2, REPS, TOK, BW), BF16),
            VMEM((TOK, ROWS), BF16),
            VMEM((REPS, 2, OWN, THIN), F32),
            VMEM((2 * HID, TOK), F32),
            VMEM((HID, TOK), F32),
            VMEM((HID, TOK), F32),
            VMEM((HID, TOK), F32),
            VMEM((2, HID, TOK), BF16),
            VMEM((TOK, HID), BF16),
            VMEM((2 * HID, TOK), BF16),
            VMEM((REPS, TOK, BW), BF16),
            VMEM((REPS, 2, SIDE - 1, BAND, HALF), BF16),
            VMEM((REPS, 2, BAND, HALF), BF16),
            VMEM((REPS, 2, 2 * SIDE - 1, OWN, THIN), BF16),
            VMEM((REPS, TOK, BW), BF16),
            VMEM((3, 2, HID, BW), BF16),
            VMEM((3, HID, BW), BF16),
            dma((2,)),
            dma((3, CUTS)),
            dma((2, 2)),
            dma((4, REPS, 2)),
            dma((4, REPS, 2)),
            dma((3 * CUTS,)),
            dma((3 * CUTS,)),
            dma((3,)),
            dma((3,)),
            dma((3 * CUTS,)),
            dma((3 * CUTS,)),
            dma((3, 2)),
            dma((3, 2)),
            dma((3, CUTS)),
            dma((3, CUTS)),
            dma((2, 3)),
            dma((3, CUTS, 2)),
        ],
        compiler_params=pltpu.CompilerParams(
            collective_id=0, has_side_effects=True, vmem_limit_bytes=63 * 2**20
        ),
        name="inner_round",
    )(in_ids, target_ids, table, targets, outer_gu, outer_down, *moments)


def hand_over_kernel(*refs):
    sources, results, (held, in_sem, out_sem) = refs[:4], refs[4:8], refs[8:]
    ins, outs = [], []
    for i in range(6):
        n, j = (i // 2 * 2, i % 2) if i < 4 else ((i - 4) * 2 + 1, None)
        source = sources[n] if j is None else sources[n].at[j]
        result = results[n] if j is None else results[n].at[j]
        ins.append(pltpu.make_async_copy(source, held.at[i], in_sem.at[i]))
        outs.append(pltpu.make_async_copy(held.at[i], result, out_sem.at[i]))
    for copy in ins:
        copy.start()
    for one, two in zip(ins, outs):
        one.wait()
        two.start()
    for copy in outs:
        copy.wait()


def hand_over(*arrays):
    anywhere = pl.BlockSpec(memory_space=pl.ANY)
    return pl.pallas_call(
        hand_over_kernel,
        out_shape=tuple(jax.ShapeDtypeStruct(array.shape, F32) for array in arrays),
        in_specs=[anywhere] * 4,
        out_specs=(anywhere,) * 4,
        scratch_shapes=[
            VMEM((6, HID, BW), F32),
            pltpu.SemaphoreType.DMA((6,)),
            pltpu.SemaphoreType.DMA((6,)),
        ],
        name="hand_over",
    )(*arrays)


def on_device(
    in_table,
    target_table,
    in_ids,
    target_ids,
    gate_up,
    down,
    mom_gate_up,
    mom_down,
    m_gate_up,
    v_gate_up,
    m_down,
    v_down,
):
    news = whole_round(
        in_ids[0],
        target_ids[0],
        in_table[0],
        target_table[0],
        jnp.swapaxes(gate_up, 1, 2),
        down,
        jnp.swapaxes(m_gate_up[0], 1, 2),
        jnp.swapaxes(v_gate_up[0], 1, 2),
        m_down[0],
        v_down[0],
        jnp.swapaxes(mom_gate_up, 1, 2),
        mom_down,
    )
    new_gu, new_down, new_mom_gu, new_mom_down = hand_over(*news)
    return (jnp.swapaxes(new_gu, 1, 2), new_down, jnp.swapaxes(new_mom_gu, 1, 2), new_mom_down)


def solution(mesh):
    in_specs = (
        P("rep", None, None),
        P("rep", None, None),
        P("rep", None, None),
        P("rep", None, None),
        P(None, "rep", "fsdp"),
        P("fsdp", "rep"),
        P(None, "rep", "fsdp"),
        P("fsdp", "rep"),
        P("rep", None, None, "fsdp"),
        P("rep", None, None, "fsdp"),
        P("rep", "fsdp", None),
        P("rep", "fsdp", None),
    )
    out_specs = (P(None, "rep", "fsdp"), P("fsdp", "rep"), P(None, "rep", "fsdp"), P("fsdp", "rep"))
    return jax.shard_map(
        on_device, mesh=mesh, in_specs=in_specs, out_specs=out_specs, check_vma=False
    )
```

```python
import math

import jax
import jax.numpy as jnp
from jax import lax
from jax.experimental import pallas as pl
from jax.experimental.pallas import tpu as pltpu
from jax.sharding import PartitionSpec as P

D = 2048
FF = 14336
STEPS = 4
TOK = 256
ROWS = 256
SHARDS = 32
HID = FF // SHARDS
SIDE = 4
REPS = 4
BW = D // REPS
BAND = TOK // SIDE
OWN = BAND // SIDE
HALF = BW // 2
THIN = HALF // 2
CUTS = 4
CUT = HID // CUTS
IN_FLIGHT = 3

beta_one = 0.9
beta_two = 0.95
inner_rate = 0.03
decay_rate = 0.1
epsilon = 1e-08
outer_rate = 0.7
momentum_rate = 0.9

in_scale = 1.0 / D**0.5
out_scale = 1.0 / FF**0.5
first_gain = inner_rate
step_gain = first_gain * (1.0 - beta_one)
second_gain = step_gain**2 / (1.0 - beta_two)
root_gain = math.sqrt(second_gain)
keep_rate = 1.0 - inner_rate * decay_rate

MESH = pl.DeviceIdType.MESH
VMEM = pltpu.VMEM
F32 = jnp.float32
BF16 = jnp.bfloat16


def adam(weight, grad, first, second, gain):
    t = grad * gain
    first = beta_one * first + t
    second = beta_two * second + t * t
    root = second * lax.rsqrt(second) + epsilon * root_gain
    move = first * pl.reciprocal(root, approx=True)
    return keep_rate * weight - root_gain * move, first, second


def dot(a, b):
    return jnp.dot(a, b, preferred_element_type=F32)


def dot_last(a, b):
    return lax.dot_general(a, b, (((1,), (1,)), ((), ())), preferred_element_type=F32)


def round_kernel(
    in_ids,
    target_ids,
    table_hbm,
    targets_hbm,
    outer_gu,
    outer_down,
    m_gu,
    v_gu,
    m_down,
    v_down,
    mom_gu,
    mom_down,
    new_gu,
    new_down,
    new_mom_gu,
    new_mom_down,
    table,
    targets,
    weight,
    first,
    second,
    start,
    narrow,
    stage,
    inputs,
    pick,
    wanted,
    gate_up_buf,
    slope_buf,
    silu_buf,
    hidden_grad,
    hidden_t,
    hidden,
    pre_grad,
    partial,
    land_one,
    sum_one,
    land_two,
    out_grad,
    land_mate,
    land_far,
    table_sem,
    load_sem,
    stage_sem,
    send_sem,
    recv_sem,
    z_send,
    z_recv,
    core_send,
    core_recv,
    fwd_send,
    fwd_recv,
    mate_send,
    mate_recv,
    far_send,
    far_recv,
    outer_sem,
    out_sem,
):
    rep = lax.axis_index("rep")
    fsdp = lax.axis_index("fsdp")
    zh, core = rep // 2, rep % 2
    zl = fsdp // (SIDE * SIDE)
    side = ((fsdp // SIDE) % SIDE, fsdp % SIDE)
    mate = (zh * 2 + (1 - core), fsdp)
    far = ((1 - zh) * 2 + core, fsdp)

    def quarter(n):
        return ((zh + n // 2) % 2) * 2 + (core + n % 2) % 2

    def cols_of(n):
        return pl.ds(pl.multiple_of(quarter(n) * BW, BW), BW)

    def peer(part, d_first, d_second, d_z):
        one = (side[part] + d_first) % SIDE
        two = (side[1 - part] + d_second) % SIDE
        z = (zl + d_z) % 2
        x, y = (one, two) if part == 0 else (two, one)
        return (rep, z * SIDE * SIDE + x * SIDE + y)

    cross = [(2, 1), (1, 1), (3, 1), (2, 0), (1, 0), (3, 0), (0, 1)]
    along = (2, 1, 3)
    partners = [mate, far]
    partners += [peer(0, o, 0, dz) for o in range(1, SIDE) for dz in range(2)]
    partners += [peer(0, 0, ds, dz) for ds, dz in cross]

    barrier = pltpu.get_barrier_semaphore()
    for other in partners:
        pl.semaphore_signal(barrier, inc=1, device_id=other, device_id_type=MESH)

    def in_rows(count, height, body, unroll=1):
        def go(i, carry):
            body(pl.ds(pl.multiple_of(i * height, height), height))
            return carry

        lax.fori_loop(0, count // height, go, 0, unroll=unroll)

    def remote(src, dst, one, two, other):
        return pltpu.make_async_remote_copy(
            src_ref=src,
            dst_ref=dst,
            send_sem=one,
            recv_sem=two,
            device_id=other,
            device_id_type=MESH,
        )

    def outer_cut(j, c):
        rows = pl.ds(c * CUT, CUT)
        source = outer_gu.at[j] if j < 2 else outer_down
        return pltpu.make_async_copy(
            source.at[rows, :], weight.at[0, j, rows, :], load_sem.at[j, c]
        )

    for j in range(3):
        for c in range(CUTS):
            outer_cut(j, c).start()
    tables = [
        pltpu.make_async_copy(source, held, table_sem.at[i])
        for i, (source, held) in enumerate(((table_hbm, table), (targets_hbm, targets)))
    ]
    for copy in tables:
        copy.start()
    blocks = [(j, n) for j in range(3) for n in range(REPS)]

    def moment_copies(i):
        j, n = blocks[i]
        sources = (m_gu.at[j], v_gu.at[j]) if j < 2 else (m_down, v_down)
        return [
            pltpu.make_async_copy(
                source.at[:, cols_of(n)], stage.at[i % 2, s], stage_sem.at[i % 2, s]
            )
            for s, source in enumerate(sources)
        ]

    for i in range(2):
        for copy in moment_copies(i):
            copy.start()

    def narrow_outer(j, c):
        outer_cut(j, c).wait()
        for r in range(0, CUT, 16):
            rows = pl.ds(c * CUT + r, 16)
            start[0, j, rows, :] = weight[0, j, rows, :].astype(BF16)

    narrow_outer(0, 0)
    pl.semaphore_wait(barrier, len(partners))

    cuts = [(j, c) for j in range(3) for c in range(CUTS)]

    def z_copy(i):
        j, c = cuts[i]
        rows = pl.ds(c * CUT, CUT)
        return remote(
            start.at[0, j, rows, :], start.at[2, j, rows, :], z_send.at[i], z_recv.at[i], far
        )

    def fwd_copy(i):
        j, c = cuts[i]
        rows = pl.ds(c * CUT, CUT)
        return remote(
            start.at[2, j, rows, :], start.at[3, j, rows, :], fwd_send.at[i], fwd_recv.at[i], mate
        )

    def core_copy(j):
        return remote(start.at[0, j], start.at[1, j], core_send.at[j], core_recv.at[j], mate)

    for j, c in cuts:
        if (j, c) != (0, 0):
            narrow_outer(j, c)
        if j * CUTS + c < IN_FLIGHT:
            z_copy(j * CUTS + c).start()
        if c == CUTS - 1:
            core_copy(j).start()

    def widen(j, n):
        def rows_of(rows):
            weight[n, j, rows, :] = start[n, j, rows, :].astype(F32)

        in_rows(HID, 16, rows_of, 2)

    def take_moments(i):
        j, n = blocks[i]
        for copy in moment_copies(i):
            copy.wait()

        def rows_of(rows):
            first[n, j, rows, :] = stage[i % 2, 0, rows, :].astype(F32) * first_gain
            second[n, j, rows, :] = stage[i % 2, 1, rows, :].astype(F32) * second_gain

        in_rows(HID, 16, rows_of, 2)
        if i + 2 < len(blocks):
            for copy in moment_copies(i + 2):
                copy.start()

    def take_cut(i):
        copy = z_copy(i)
        copy.wait_recv()
        fwd_copy(i).start()
        copy.wait_send()
        if i + IN_FLIGHT < len(cuts):
            z_copy(i + IN_FLIGHT).start()

    def chosen_t(ids, k):
        rows = lax.broadcasted_iota(jnp.int32, (ROWS, TOK), 0)
        return (ids[pl.ds(k, 1), :] == rows).astype(F32)

    def look_up_inputs(k, slot):
        chosen = chosen_t(in_ids, k).T.astype(BF16)
        for n in range(REPS):
            inputs[slot, n] = dot(chosen, table[:, cols_of(n)]).astype(BF16)

    def band(coordinate):
        return pl.ds(pl.multiple_of(coordinate * BAND, BAND), BAND)

    def own_rows(one, two):
        return pl.ds(pl.multiple_of(one * BAND + two * OWN, OWN), OWN)

    def thin_cols(base, z):
        return pl.ds(pl.multiple_of(base + z * THIN, THIN), THIN)

    def send(kind, n, h, src, dst, other):
        remote(src, dst, send_sem.at[kind, n, h], recv_sem.at[kind, n, h], other).start()

    def wait_bytes(kind, n, h, sem):
        like = land_one.at[n, h] if kind in (0, 3) else land_two.at[n, h]
        pltpu.make_async_copy(like, like, sem.at[kind, n, h]).wait()

    def scatter_one(n, held):
        partial[n] = (dot(hidden[...], held[n, 2]) * out_scale).astype(BF16)
        for h in range(2):
            cols = pl.ds(h * HALF, HALF)
            for o in along:
                src = partial.at[n, band((side[h] + o) % SIDE), cols]
                send(0, n, h, src, land_one.at[n, h, o - 1], peer(h, o, 0, 0))

    def scatter_two(n):
        for h in range(2):
            wait_bytes(0, n, h, recv_sem)
            total = partial[n, band(side[h]), pl.ds(h * HALF, HALF)].astype(F32)
            for o in range(SIDE - 1):
                total = total + land_one[n, h, o].astype(F32)
            sum_one[n, h] = total.astype(BF16)
            for i, (ds, dz) in enumerate(cross):
                to = (side[1 - h] + ds) % SIDE
                rows = pl.ds(pl.multiple_of(to * OWN, OWN), OWN)
                src = sum_one.at[n, h, rows, thin_cols(0, (zl + dz) % 2)]
                send(1, n, h, src, land_two.at[n, h, i], peer(h, 0, ds, dz))

    def gather_one(n):
        for h in range(2):
            wait_bytes(1, n, h, recv_sem)
            rows = pl.ds(pl.multiple_of(side[1 - h] * OWN, OWN), OWN)
            total = sum_one[n, h, rows, thin_cols(0, zl)].astype(F32)
            for i in range(len(cross)):
                total = total + land_two[n, h, i].astype(F32)
            mine = (n, own_rows(side[h], side[1 - h]), thin_cols(h * HALF, zl))
            out_grad[mine] = ((total - wanted[n, h]) * (1.0 / TOK)).astype(BF16)
            for ds, dz in cross:
                send(2, n, h, out_grad.at[mine], out_grad.at[mine], peer(h, 0, ds, dz))

    def gather_two(n):
        for h in range(2):
            wait_bytes(2, n, h, recv_sem)
            mine = out_grad.at[n, band(side[h]), pl.ds(h * HALF, HALF)]
            for o in along:
                send(3, n, h, mine, mine, peer(h, o, 0, 0))

    def update(n, j, product, last):
        gain = step_gain * (in_scale if j < 2 else out_scale)
        for r in range(0, HID, 16):
            here = (n, j, pl.ds(r, 16), slice(None))
            w, m, v = adam(weight[here], product[r : r + 16, :], first[here], second[here], gain)
            if last:
                narrow[here] = (start[here].astype(F32) - w).astype(BF16)
            else:
                weight[here] = w
                first[here] = m
                second[here] = v
                narrow[here] = w.astype(BF16)

    def use_block(n, held, fresh):
        for h in range(2):
            wait_bytes(3, n, h, recv_sem)
        product = dot_last(held[n, 2], out_grad[n])
        if fresh:
            hidden_grad[...] = product
        else:
            hidden_grad[...] += product

    def update_down(n, slot, last):
        update(n, 2, dot(hidden_t[slot], out_grad[n]), last)

    def update_gu(n, slot, last):
        product = dot(pre_grad[...], inputs[slot, n])
        for j in range(2):
            update(n, j, product[j * HID : (j + 1) * HID, :], last)

    def update_all_gu(slot):
        for n in range(REPS):
            update_gu(n, slot, False)

    def update_late(slot):
        for n in range(2):
            update_down(n, slot, False)

    def forward(held, slot):
        both = [held[n, 0:2].reshape(2 * HID, BW) for n in range(REPS)]
        rows_in = jnp.concatenate([inputs[slot, n] for n in range(REPS)], axis=1)
        gate_up_buf[...] = dot_last(jnp.concatenate(both, axis=1), rows_in)
        for r in range(0, HID, 16):
            rows = pl.ds(r, 16)
            gate = gate_up_buf[rows, :] * in_scale
            upper = gate_up_buf[pl.ds(HID + r, 16), :] * in_scale
            sigmoid = jax.nn.sigmoid(gate)
            silu = gate * sigmoid
            hidden_t[slot, rows, :] = (silu * upper).astype(BF16)
            silu_buf[rows, :] = silu * out_scale
            slope_buf[rows, :] = upper * sigmoid * (1.0 + gate * (1.0 - sigmoid)) * out_scale
        hidden[...] = hidden_t[slot].T

    def look_up_targets(k):
        pick[...] = chosen_t(target_ids, k).T.astype(BF16)
        for n in range(REPS):
            for h in range(2):
                rows = own_rows(side[h], side[1 - h])
                cols = thin_cols(quarter(n) * BW + h * HALF, zl)
                wanted[n, h] = dot(pick[rows, :], targets[:, cols])

    def backward():
        pre_grad[:HID, :] = (hidden_grad[...] * slope_buf[...]).astype(BF16)
        pre_grad[HID:, :] = (hidden_grad[...] * silu_buf[...]).astype(BF16)

    def end_sends():
        for n in range(REPS):
            for kind in range(4):
                for h in range(2):
                    wait_bytes(kind, n, h, send_sem)

    for copy in tables:
        copy.wait()
    look_up_inputs(0, 0)
    for j in range(3):
        widen(j, 0)
    for i in range(2 * CUTS):
        take_moments(i)
        take_cut(i)
    for j in range(2):
        core_copy(j).wait_recv()
        widen(j, 1)
    for i in range(2 * CUTS):
        fwd_copy(i).wait_recv()
    forward(start, 0)
    core_copy(2).wait_recv()
    scatter_one(0, start)
    scatter_one(1, start)
    look_up_targets(0)
    take_cut(8)
    take_moments(8)
    scatter_two(0)
    scatter_two(1)
    take_cut(9)
    widen(2, 1)
    gather_one(0)
    gather_one(1)
    take_cut(10)
    take_moments(9)
    take_cut(11)
    for i in range(2 * CUTS, 3 * CUTS):
        fwd_copy(i).wait_recv()
    scatter_one(2, start)
    scatter_one(3, start)
    take_moments(10)
    take_moments(11)
    look_up_inputs(1, 1)
    scatter_two(2)
    scatter_two(3)
    gather_two(0)
    gather_two(1)
    for j in range(2):
        widen(j, 2)
        widen(j, 3)
    gather_one(2)
    gather_one(3)
    widen(2, 2)
    widen(2, 3)
    use_block(0, start, True)
    use_block(1, start, False)
    gather_two(2)
    gather_two(3)
    for n in (2, 3):
        use_block(n, start, False)
        update_down(n, 0, False)
    backward()
    update_all_gu(0)
    end_sends()

    def middle(k, slot, order, last):
        a, b, c, d = order
        forward(narrow, slot)
        scatter_one(a, narrow)
        scatter_one(b, narrow)
        update_late(1 - slot)
        if last:
            look_up_targets(k)
            for n in (a, b):
                scatter_two(n)
            for n in (c, d):
                scatter_one(n, narrow)
            for n in (a, b):
                gather_one(n)
            for n in (c, d):
                scatter_two(n)
            for n in (a, b):
                gather_two(n)
            for n in (c, d):
                gather_one(n)
            use_block(a, narrow, True)
            update_down(a, slot, True)
            return
        scatter_one(c, narrow)
        scatter_one(d, narrow)
        look_up_targets(k)
        look_up_inputs(k + 1, 1 - slot)
        for stage_of in (scatter_two, gather_one, gather_two):
            for n in order:
                stage_of(n)
        use_block(a, narrow, True)
        update_down(a, slot, False)

    def step(k, carry):
        slot = k % 2
        middle(k, slot, (2, 3, 0, 1), False)
        use_block(3, narrow, False)
        update_down(3, slot, False)
        use_block(0, narrow, False)
        use_block(1, narrow, False)
        backward()
        update_all_gu(slot)
        end_sends()
        return carry

    lax.fori_loop(1, STEPS - 1, step, 0)

    def mate_copy(j, n):
        return remote(
            narrow.at[n, j],
            land_mate.at[j, n // 2],
            mate_send.at[j, n // 2],
            mate_recv.at[j, n // 2],
            mate,
        )

    def far_copy(j, c):
        rows = pl.ds(c * CUT, CUT)
        return remote(
            narrow.at[2, j, rows, :], land_far.at[j, rows, :], far_send.at[j, c], far_recv.at[j, c], far
        )

    def pair_sum(j):
        mate_copy(j, 3).wait_recv()
        for c in range(CUTS):
            def rows_of(r):
                rows = pl.ds(pl.multiple_of(c * CUT + r * 16, 16), 16)
                both = narrow[2, j, rows, :].astype(F32) + land_mate[j, 1, rows, :].astype(F32)
                narrow[2, j, rows, :] = both.astype(BF16)

            for r in range(CUT // 16):
                rows_of(r)
            far_copy(j, c).start()

    outer_loads = [
        pltpu.make_async_copy(source.at[j] if j < 2 else flat, held.at[3, j], outer_sem.at[i, j])
        for i, (source, flat, held) in enumerate(
            ((outer_gu, outer_down, first), (mom_gu, mom_down, second))
        )
        for j in range(3)
    ]
    slot = (STEPS - 1) % 2
    middle(STEPS - 1, slot, (3, 2, 0, 1), True)
    mate_copy(2, 3).start()
    use_block(2, narrow, False)
    update_down(2, slot, True)
    gather_two(0)
    gather_two(1)
    pair_sum(2)
    use_block(0, narrow, False)
    use_block(1, narrow, False)
    backward()
    update_gu(3, slot, True)
    for j in range(2):
        mate_copy(j, 3).start()
    for copy in outer_loads:
        copy.start()
    update_gu(2, slot, True)
    for j in range(2):
        pair_sum(j)
    update_down(1, slot, True)
    mate_copy(2, 1).start()
    update_gu(1, slot, True)
    for j in range(2):
        mate_copy(j, 1).start()
    update_down(0, slot, True)
    update_gu(0, slot, True)
    end_sends()

    def out_copies(j, c):
        rows = pl.ds(c * CUT, CUT)
        outs = (new_gu.at[j], new_mom_gu.at[j]) if j < 2 else (new_down, new_mom_down)
        return [
            pltpu.make_async_copy(
                weight.at[i, j, rows, :], out.at[rows, :], out_sem.at[j, c, i]
            )
            for i, out in enumerate(outs)
        ]

    for copy in outer_loads:
        copy.wait()
    for j in (2, 0, 1):
        mate_copy(j, 1).wait_recv()
        for c in range(CUTS):
            far_copy(j, c).wait_recv()
            for r in range(CUT // 16):
                rows = pl.ds(c * CUT + r * 16, 16)
                total = (
                    narrow[0, j, rows, :].astype(F32)
                    + land_mate[j, 0, rows, :].astype(F32)
                    + land_far[j, rows, :].astype(F32)
                )
                mean = total / REPS
                new_mom = momentum_rate * second[3, j, rows, :] + mean
                weight[1, j, rows, :] = new_mom
                weight[0, j, rows, :] = first[3, j, rows, :] - outer_rate * (
                    mean + momentum_rate * new_mom
                )
            for copy in out_copies(j, c):
                copy.start()

    for j in range(3):
        core_copy(j).wait_send()
        for n in (1, 3):
            mate_copy(j, n).wait_send()
        for c in range(CUTS):
            far_copy(j, c).wait_send()
            for copy in out_copies(j, c):
                copy.wait()
    for i in range(len(cuts)):
        fwd_copy(i).wait_send()


def whole_round(in_ids, target_ids, table, targets, outer_gu, outer_down, *moments):
    in_vmem = pl.BlockSpec(memory_space=VMEM)
    anywhere = pl.BlockSpec(memory_space=pl.ANY)
    every = (REPS, 3, HID, BW)
    dma = pltpu.SemaphoreType.DMA
    gu_shape = jax.ShapeDtypeStruct((2, HID, BW), F32)
    down_shape = jax.ShapeDtypeStruct((HID, BW), F32)
    return pl.pallas_call(
        round_kernel,
        out_shape=(gu_shape, down_shape, gu_shape, down_shape),
        in_specs=[in_vmem] * 2 + [anywhere] * 10,
        out_specs=(anywhere,) * 4,
        scratch_shapes=[
            VMEM((ROWS, D), BF16),
            VMEM((ROWS, D), BF16),
            VMEM(every, F32),
            VMEM(every, F32),
            VMEM(every, F32),
            VMEM(every, BF16),
            VMEM(every, BF16),
            VMEM((2, 2, HID, BW), BF16),
            VMEM((2, REPS, TOK, BW), BF16),
            VMEM((TOK, ROWS), BF16),
            VMEM((REPS, 2, OWN, THIN), F32),
            VMEM((2 * HID, TOK), F32),
            VMEM((HID, TOK), F32),
            VMEM((HID, TOK), F32),
            VMEM((HID, TOK), F32),
            VMEM((2, HID, TOK), BF16),
            VMEM((TOK, HID), BF16),
            VMEM((2 * HID, TOK), BF16),
            VMEM((REPS, TOK, BW), BF16),
            VMEM((REPS, 2, SIDE - 1, BAND, HALF), BF16),
            VMEM((REPS, 2, BAND, HALF), BF16),
            VMEM((REPS, 2, 2 * SIDE - 1, OWN, THIN), BF16),
            VMEM((REPS, TOK, BW), BF16),
            VMEM((3, 2, HID, BW), BF16),
            VMEM((3, HID, BW), BF16),
            dma((2,)),
            dma((3, CUTS)),
            dma((2, 2)),
            dma((4, REPS, 2)),
            dma((4, REPS, 2)),
            dma((3 * CUTS,)),
            dma((3 * CUTS,)),
            dma((3,)),
            dma((3,)),
            dma((3 * CUTS,)),
            dma((3 * CUTS,)),
            dma((3, 2)),
            dma((3, 2)),
            dma((3, CUTS)),
            dma((3, CUTS)),
            dma((2, 3)),
            dma((3, CUTS, 2)),
        ],
        compiler_params=pltpu.CompilerParams(
            collective_id=0, has_side_effects=True, vmem_limit_bytes=63 * 2**20
        ),
        name="inner_round",
    )(in_ids, target_ids, table, targets, outer_gu, outer_down, *moments)


def hand_over_kernel(*refs):
    sources, results, (held, in_sem, out_sem) = refs[:4], refs[4:8], refs[8:]
    ins, outs = [], []
    for i in range(6):
        n, j = (i // 2 * 2, i % 2) if i < 4 else ((i - 4) * 2 + 1, None)
        source = sources[n] if j is None else sources[n].at[j]
        result = results[n] if j is None else results[n].at[j]
        ins.append(pltpu.make_async_copy(source, held.at[i], in_sem.at[i]))
        outs.append(pltpu.make_async_copy(held.at[i], result, out_sem.at[i]))
    for copy in ins:
        copy.start()
    for one, two in zip(ins, outs):
        one.wait()
        two.start()
    for copy in outs:
        copy.wait()


def hand_over(*arrays):
    anywhere = pl.BlockSpec(memory_space=pl.ANY)
    return pl.pallas_call(
        hand_over_kernel,
        out_shape=tuple(jax.ShapeDtypeStruct(array.shape, F32) for array in arrays),
        in_specs=[anywhere] * 4,
        out_specs=(anywhere,) * 4,
        scratch_shapes=[
            VMEM((6, HID, BW), F32),
            pltpu.SemaphoreType.DMA((6,)),
            pltpu.SemaphoreType.DMA((6,)),
        ],
        name="hand_over",
    )(*arrays)


def on_device(
    in_table,
    target_table,
    in_ids,
    target_ids,
    gate_up,
    down,
    mom_gate_up,
    mom_down,
    m_gate_up,
    v_gate_up,
    m_down,
    v_down,
):
    news = whole_round(
        in_ids[0],
        target_ids[0],
        in_table[0],
        target_table[0],
        jnp.swapaxes(gate_up, 1, 2),
        down,
        jnp.swapaxes(m_gate_up[0], 1, 2),
        jnp.swapaxes(v_gate_up[0], 1, 2),
        m_down[0],
        v_down[0],
        jnp.swapaxes(mom_gate_up, 1, 2),
        mom_down,
    )
    new_gu, new_down, new_mom_gu, new_mom_down = hand_over(*news)
    return (jnp.swapaxes(new_gu, 1, 2), new_down, jnp.swapaxes(new_mom_gu, 1, 2), new_mom_down)


def solution(mesh):
    in_specs = (
        P("rep", None, None),
        P("rep", None, None),
        P("rep", None, None),
        P("rep", None, None),
        P(None, "rep", "fsdp"),
        P("fsdp", "rep"),
        P(None, "rep", "fsdp"),
        P("fsdp", "rep"),
        P("rep", None, None, "fsdp"),
        P("rep", None, None, "fsdp"),
        P("rep", "fsdp", None),
        P("rep", "fsdp", None),
    )
    out_specs = (P(None, "rep", "fsdp"), P("fsdp", "rep"), P(None, "rep", "fsdp"), P("fsdp", "rep"))
    return jax.shard_map(
        on_device, mesh=mesh, in_specs=in_specs, out_specs=out_specs, check_vma=False
    )
```
